512 devices in a mesh: rad: 32 (over x, y), ang: 16 (over z, core).
Axes of the slice: x: 4, y: 8, z: 8, core: 2. Of those that a mesh axis runs over, the one named last changes fastest.
Arguments:
- field: bfloat16 [512, 1024, 2048], P('rad', 'ang'), may hold values from -48 to 48
- start: float32 [512, 128], replicated, may hold values from -6 to 6
Outputs:
- core: bfloat16 [128, 1024, 2048], P(None, ('ang', 'rad'))
The draws below stay inside these ranges and needn't reach their ends.
All inputs are finite; a program needn't handle non-finite values.
Results may differ from the reference program's by a relative error of at most 0.004.
The reference program's roundings to bfloat16 on the way (of `unfold` and `narrow`) count: a program that leaves them out, or rounds other values in their place, can miss the bound.
Values may be sent and summed in bfloat16 or wider, within the bound.
No kernel may reach another device: no remote copies, remote signals or barrier semaphores. Data moves between devices by JAX's collectives and lax.ppermute only.
A program may use at most 64 MiB of HBM per device.

```python
import math
import jax
import jax.numpy as jnp
from jax import lax

NR = 512
RANK = 128
NPH = 2048
ITERS = 2
NTH = 1024


def draw_field(key, part):
    key = jax.random.fold_in(key, 11)
    noise_key = jax.random.fold_in(key, 0)
    scale_key = jax.random.fold_in(key, 1)
    couple_key = jax.random.fold_in(key, 2)
    sign_key = jax.random.fold_in(key, 4)
    scale = jnp.exp(jax.random.uniform(scale_key, (NR, 1, 1), jnp.float32) * math.log(2.0))
    couple = jax.random.uniform(couple_key, (1, NTH, 1), jnp.float32, 0.3, 0.9)
    noise = jnp.clip(jax.random.normal(noise_key, (NR + 1, NTH, NPH), jnp.float32), -5.0, 5.0)
    values = scale * (noise[:-1] + couple * noise[1:])
    radius_of = jnp.arange(NTH) % NR
    marked = (jnp.arange(NR)[:, None] == radius_of[None, :]).astype(jnp.float32)[:, :, None]
    signs = jnp.where(jax.random.bernoulli(sign_key, 0.5, (1, NTH, NPH)), 1.0, -1.0).astype(jnp.float32)
    values = values + 20.0 * marked * signs
    return values.astype(jnp.bfloat16)


def scatter_about(own_key, dims, deviation, bound, held_as=jnp.bfloat16):
    return jnp.clip(deviation * jax.random.normal(own_key, dims, jnp.float32), -bound, bound).astype(held_as)


def setup_inputs(seed: int = 0) -> dict:
    splits = jax.random.split(jax.random.key(seed), 3)
    return {
        "field": draw_field(jax.random.fold_in(splits[2], 71), 0),
        "start": scatter_about(splits[1], (NR, RANK), 1.0, 6.0, jnp.float32),
    }


def orthonormal(grown):
    inner = jnp.dot(grown.T, grown, precision=lax.Precision.HIGHEST)
    lower = jnp.linalg.cholesky(inner)
    return lax.linalg.triangular_solve(lower, grown, left_side=False, lower=True, transpose_a=True)

def subspace(gram, start):
    basis = start
    for step in range(ITERS):
        basis = orthonormal(jnp.dot(gram, basis, precision=lax.Precision.HIGHEST))
    return basis

def reference(field, start):
    unfold = field.reshape(NR, NTH * NPH)
    gram = jnp.dot(unfold.astype(jnp.float32), unfold.T.astype(jnp.float32), preferred_element_type=jnp.float32)
    narrow = subspace(gram, start).astype(jnp.bfloat16)
    core = jnp.dot(narrow.T.astype(jnp.float32), unfold.astype(jnp.float32), preferred_element_type=jnp.float32)
    return core.astype(jnp.bfloat16).reshape(RANK, NTH, NPH)
```

```python
import functools

import jax
import jax.numpy as jnp
from jax import lax
from jax.experimental import pallas as pl
from jax.experimental.pallas import tpu as pltpu
from jax.sharding import Mesh, PartitionSpec as P

ITERS = 2
SUB = 8
TILE = 128
AXES = ("x", "y", "z", "core")
SIZES = (4, 8, 8, 2)
RAD = ("x", "y")
WIDE = ("x", "z")
MID = ("y", "core")
VMEM_LIMIT = 48 * 2**20


def group(names):
    size = 1
    for name in names:
        size *= SIZES[AXES.index(name)]
    return size


def pairs(parts):
    return [(i, j) for i in range(parts) for j in range(i, parts)]


def gram_kernel(u_ref, out_ref, acc_ref):
    step = pl.program_id(0) * pl.num_programs(1) + pl.program_id(1)
    last = pl.num_programs(0) * pl.num_programs(1) - 1
    src, _, radii, cells = u_ref.shape
    u = u_ref[...].reshape(src * radii, cells)
    half = src * radii // 2

    def outer(a, b):
        return lax.dot_general(a, b, (((1,), (1,)), ((), ())), preferred_element_type=jnp.float32)

    top = outer(u[:half], u)
    low = outer(u[half:], u[half:])

    @pl.when(step == 0)
    def _():
        acc_ref[:half] = top
        acc_ref[half:, half:] = low

    @pl.when(step > 0)
    def _():
        acc_ref[:half] += top
        acc_ref[half:, half:] += low

    @pl.when(step == last)
    def _():
        for n, (i, j) in enumerate(pairs(src * radii // TILE)):
            out_ref[n] = acc_ref[TILE * i:TILE * (i + 1), TILE * j:TILE * (j + 1)]


def partial_gram(regrouped):
    src, th, radii, ph = regrouped.shape
    order = src * radii
    cells = 1024
    count = len(pairs(order // TILE))
    return pl.pallas_call(
        gram_kernel,
        grid=(th, ph // cells),
        in_specs=[pl.BlockSpec((src, 1, radii, cells), lambda t, c: (0, t, 0, c))],
        out_specs=pl.BlockSpec((count, TILE, TILE), lambda t, c: (0, 0, 0)),
        out_shape=jax.ShapeDtypeStruct((count, TILE, TILE), jnp.float32),
        scratch_shapes=[pltpu.VMEM((order, order), jnp.float32)],
        compiler_params=pltpu.CompilerParams(vmem_limit_bytes=VMEM_LIMIT),
        cost_estimate=pl.CostEstimate(flops=2 * order * order * th * ph, bytes_accessed=2 * order * th * ph, transcendentals=0),
        name="gram",
    )(regrouped)


def sum_kernel(x_ref, out_ref):
    total = x_ref[0]
    for n in range(1, x_ref.shape[0]):
        total = total + x_ref[n]
    out_ref[...] = jnp.broadcast_to(total[None], out_ref.shape)


def sum_and_repeat(x, copies):
    return pl.pallas_call(
        sum_kernel,
        in_specs=[pl.BlockSpec(memory_space=pltpu.VMEM)],
        out_specs=pl.BlockSpec(memory_space=pltpu.VMEM),
        out_shape=jax.ShapeDtypeStruct((copies,) + x.shape[1:], jnp.float32),
        name="total",
    )(x)


def swap(x, names):
    return lax.all_to_all(x, names, split_axis=0, concat_axis=0, tiled=True)


def sum_everywhere(blocks):
    wide, mid = group(WIDE), group(MID)
    pieces = blocks.reshape(wide, -1, TILE)
    share = sum_and_repeat(swap(pieces, WIDE), mid)
    share = sum_and_repeat(swap(share, MID), wide)
    return swap(share, WIDE).reshape(blocks.shape)


def inverse_lower(inner):
    n = inner.shape[0]
    parts = n // SUB
    row = lax.broadcasted_iota(jnp.int32, (SUB, n), 0)
    col = lax.broadcasted_iota(jnp.int32, (SUB, n), 1)
    left = [inner[SUB * q:SUB * (q + 1)] for q in range(parts)]
    right = [jnp.where(col == row + SUB * q, 1.0, 0.0) for q in range(parts)]

    def spread(x, c):
        return jnp.broadcast_to(x[:, c:c + 1], (SUB, n))

    def pick(x, r):
        return jnp.broadcast_to(x[r:r + 1], (SUB, n))

    for p in range(parts):
        columns = {q: [spread(left[q], SUB * p + j) for j in range(SUB)] for q in range(p, parts)}
        pivots = jnp.ones((SUB, n), jnp.float32)
        for j in range(SUB):
            own = columns[p]
            pivot = pick(own[j], j)
            inv = 1.0 / pivot
            pivots = jnp.where(row == j, pivot, pivots)
            lead_left = pick(left[p], j)
            lead_right = pick(right[p], j)
            lead = [pick(own[c], j) for c in range(j + 1, SUB)]
            for q in range(p, parts):
                times = columns[q][j] * inv
                if q == p:
                    times = jnp.where(row > j, times, 0.0)
                left[q] = left[q] - times * lead_left
                right[q] = right[q] - times * lead_right
                for c in range(j + 1, SUB):
                    columns[q][c] = columns[q][c] - times * lead[c - j - 1]
        right[p] = right[p] / jnp.sqrt(pivots)
    return jnp.concatenate(right, axis=0)


def exact(a, b, dims):
    return lax.dot_general(
        a, b, ((dims[:1], dims[1:]), ((), ())),
        precision=lax.Precision.HIGHEST, preferred_element_type=jnp.float32,
    )


def core_kernel(blocks_ref, start_ref, u_ref, out_ref, gram_ref, basis_ref, held_ref, sem):
    copy = pltpu.make_async_copy(u_ref, held_ref, sem)
    copy.start()
    order = start_ref.shape[0]
    for n, (i, j) in enumerate(pairs(order // TILE)):
        block = blocks_ref[n]
        gram_ref[TILE * i:TILE * (i + 1), TILE * j:TILE * (j + 1)] = block
        if i != j:
            gram_ref[TILE * j:TILE * (j + 1), TILE * i:TILE * (i + 1)] = block.T
    basis_ref[...] = start_ref[...]

    def step(_, carry):
        grown = exact(gram_ref[...], basis_ref[...], (1, 0))
        inner = exact(grown, grown, (0, 0))
        basis_ref[...] = exact(grown, inverse_lower(inner), (1, 1))
        return carry

    lax.fori_loop(0, ITERS, step, 0)
    narrow = basis_ref[...].astype(jnp.bfloat16)
    copy.wait()
    src, th, radii, ph = held_ref.shape
    cells = 512
    for t in range(th):
        for c in range(ph // cells):
            u = held_ref[:, t, :, cells * c:cells * (c + 1)].reshape(src * radii, cells)
            core = lax.dot_general(narrow, u, (((0,), (0,)), ((), ())), preferred_element_type=jnp.float32)
            out_ref[:, t * ph + cells * c:t * ph + cells * (c + 1)] = core.astype(jnp.bfloat16)


def core_of(blocks, start, regrouped):
    order, rank = start.shape
    src, th, radii, ph = regrouped.shape
    vmem = pl.BlockSpec(memory_space=pltpu.VMEM)
    return pl.pallas_call(
        core_kernel,
        in_specs=[vmem, vmem, pl.BlockSpec(memory_space=pl.ANY)],
        out_specs=vmem,
        out_shape=jax.ShapeDtypeStruct((rank, th * ph), jnp.bfloat16),
        scratch_shapes=[
            pltpu.VMEM((order, order), jnp.float32),
            pltpu.VMEM((order, rank), jnp.float32),
            pltpu.VMEM(regrouped.shape, jnp.bfloat16),
            pltpu.SemaphoreType.DMA,
        ],
        compiler_params=pltpu.CompilerParams(vmem_limit_bytes=VMEM_LIMIT),
        name="subspace_and_core",
    )(blocks, start, regrouped)


def on_device(field, start):
    radii, th, ph = field.shape
    owners = group(RAD)
    sent = field.transpose(1, 0, 2).reshape(owners, th // owners, radii, ph)
    regrouped = swap(sent, RAD)
    blocks = sum_everywhere(partial_gram(regrouped))
    core = core_of(blocks, start, regrouped)
    return core.reshape(start.shape[1], th // owners, ph)


def solution(mesh):
    fine = Mesh(mesh.devices.reshape(SIZES), AXES)
    return jax.shard_map(
        on_device,
        mesh=fine,
        in_specs=(P(RAD, ("z", "core"), None), P()),
        out_specs=P(None, ("z", "core") + RAD, None),
        check_vma=False,
    )
```

```python
import jax
import jax.numpy as jnp
from jax import lax
from jax.experimental import pallas as pl
from jax.experimental.pallas import tpu as pltpu
from jax.sharding import Mesh, PartitionSpec as P

ITERS = 2
SUB = 8
TILE = 128
AXES = ("x", "y", "z", "core")
SIZES = (4, 8, 8, 2)
RAD = ("x", "y")
WIDE = ("x", "z")
MID = ("y",)
VMEM_LIMIT = 24 * 2**20


def group(names):
    size = 1
    for name in names:
        size *= SIZES[AXES.index(name)]
    return size


def halves():
    return (((0, 1), (0, 2), (0, 3)), (0, 1)), (((1, 2), (1, 3), (2, 3)), (2, 3))


def tile_iota():
    return (lax.broadcasted_iota(jnp.int32, (TILE, TILE), d) for d in (0, 1))


def gram_kernel(u_ref, keep_ref, send_ref, acc_ref):
    src, th, radii, ph = u_ref.shape
    order = src * radii
    half = order // 2
    cells = 1024
    for t in range(th):
        for c in range(ph // cells):
            u = u_ref[:, t, :, cells * c:cells * (c + 1)].reshape(order, cells)
            top = lax.dot_general(u[:half], u, (((1,), (1,)), ((), ())), preferred_element_type=jnp.float32)
            low = lax.dot_general(u[half:], u[half:], (((1,), (1,)), ((), ())), preferred_element_type=jnp.float32)
            if t == 0 and c == 0:
                acc_ref[:half] = top
                acc_ref[half:, half:] = low
            else:
                acc_ref[:half] += top
                acc_ref[half:, half:] += low
    row, col = tile_iota()

    def block(i, j):
        return acc_ref[TILE * i:TILE * (i + 1), TILE * j:TILE * (j + 1)]

    def pack(ref, part):
        offs, (first, second) = part
        for n, (i, j) in enumerate(offs):
            ref[TILE * n:TILE * (n + 1)] = block(i, j)
        under = block(first, first)
        ref[TILE * 3:TILE * 4] = jnp.where(row > col, under, block(second, second))
        diagonal = jnp.sum(jnp.where(row == col, under, 0.0), axis=0, keepdims=True)
        ref[TILE * 4:] = jnp.broadcast_to(diagonal, (ref.shape[0] - TILE * 4, TILE))

    core = lax.axis_index("core")
    for own in (0, 1):
        @pl.when(core == own)
        def _():
            pack(keep_ref, halves()[own])
            pack(send_ref, halves()[1 - own])


def partial_gram(regrouped):
    src, th, radii, ph = regrouped.shape
    order = src * radii
    vmem = pl.BlockSpec(memory_space=pltpu.VMEM)
    out = jax.ShapeDtypeStruct((4 * TILE + group(WIDE), TILE), jnp.float32)
    return pl.pallas_call(
        gram_kernel,
        in_specs=[vmem],
        out_specs=[vmem, vmem],
        out_shape=[out, out],
        scratch_shapes=[pltpu.VMEM((order, order), jnp.float32)],
        compiler_params=pltpu.CompilerParams(vmem_limit_bytes=VMEM_LIMIT),
        name="gram",
    )(regrouped)


def unpack_half(packed, part, gram_ref):
    offs, (first, second) = part
    row, col = tile_iota()

    def put(i, j, value):
        gram_ref[TILE * i:TILE * (i + 1), TILE * j:TILE * (j + 1)] = value

    for n, (i, j) in enumerate(offs):
        value = packed[TILE * n:TILE * (n + 1)]
        put(i, j, value)
        put(j, i, value.T)
    shared = packed[TILE * 3:TILE * 4]
    diagonal = jnp.broadcast_to(packed[TILE * 4:TILE * 4 + 1], (TILE, TILE))
    turned = shared.T
    put(first, first, jnp.where(row > col, shared, jnp.where(row < col, turned, diagonal)))
    put(second, second, jnp.where(row > col, turned, shared))


def swap(x, names):
    return lax.all_to_all(x, names, split_axis=0, concat_axis=0, tiled=True)


def swap_core(x):
    return lax.ppermute(x, "core", [(0, 1), (1, 0)])


def repeat(x, copies):
    return jnp.broadcast_to(x[None], (copies,) + x.shape)


def sum_everywhere(keep, send):
    half = keep + swap_core(send)
    share = jnp.sum(swap(half.reshape(group(WIDE), 1, -1), WIDE), axis=0)
    share = jnp.sum(swap(repeat(share, group(MID)), MID), axis=0)
    mine = swap(repeat(share, group(WIDE)), WIDE).reshape(half.shape)
    return mine, swap_core(mine)


def inverse_lower(inner):
    n = inner.shape[0]
    parts = n // SUB
    row = lax.broadcasted_iota(jnp.int32, (SUB, n), 0)
    col = lax.broadcasted_iota(jnp.int32, (SUB, n), 1)
    left = [inner[SUB * q:SUB * (q + 1)] for q in range(parts)]
    right = [jnp.where(col == row + SUB * q, 1.0, 0.0) for q in range(parts)]

    def spread(x, c):
        return jnp.broadcast_to(x[:, c:c + 1], (SUB, n))

    def pick(x, r):
        return jnp.broadcast_to(x[r:r + 1], (SUB, n))

    for p in range(parts):
        columns = {q: [spread(left[q], SUB * p + j) for j in range(SUB)] for q in range(p, parts)}
        pivots = jnp.ones((SUB, n), jnp.float32)
        for j in range(SUB):
            own = columns[p]
            pivot = pick(own[j], j)
            inv = 1.0 / pivot
            pivots = jnp.where(row == j, pivot, pivots)
            lead_left = pick(left[p], j)
            lead_right = pick(right[p], j)
            lead = [pick(own[c], j) for c in range(j + 1, SUB)]
            for q in range(p, parts):
                times = columns[q][j] * inv
                if q == p:
                    times = jnp.where(row > j, times, 0.0)
                left[q] = left[q] - times * lead_left
                right[q] = right[q] - times * lead_right
                for c in range(j + 1, SUB):
                    columns[q][c] = columns[q][c] - times * lead[c - j - 1]
        right[p] = right[p] / jnp.sqrt(pivots)
    return jnp.concatenate(right, axis=0)


def exact(a, b, dims):
    return lax.dot_general(
        a, b, ((dims[:1], dims[1:]), ((), ())),
        precision=lax.Precision.HIGHEST, preferred_element_type=jnp.float32,
    )


def core_kernel(mine_ref, other_ref, start_ref, u_ref, out_ref, gram_ref, basis_ref):
    core = lax.axis_index("core")
    for own in (0, 1):
        @pl.when(core == own)
        def _():
            unpack_half(mine_ref[...], halves()[own], gram_ref)
            unpack_half(other_ref[...], halves()[1 - own], gram_ref)
    basis_ref[...] = start_ref[...]

    def step(_, carry):
        grown = exact(gram_ref[...], basis_ref[...], (1, 0))
        inner = exact(grown, grown, (0, 0))
        basis_ref[...] = exact(grown, inverse_lower(inner), (1, 1))
        return carry

    lax.fori_loop(0, ITERS, step, 0)
    narrow = basis_ref[...].T.astype(jnp.bfloat16)
    src, th, radii, ph = u_ref.shape
    cells = 512
    for t in range(th):
        for c in range(ph // cells):
            u = u_ref[:, t, :, cells * c:cells * (c + 1)].reshape(src * radii, cells)
            core = jnp.dot(narrow, u, preferred_element_type=jnp.float32)
            out_ref[:, t * ph + cells * c:t * ph + cells * (c + 1)] = core.astype(jnp.bfloat16)


def core_of(mine, other, start, regrouped):
    order, rank = start.shape
    src, th, radii, ph = regrouped.shape
    vmem = pl.BlockSpec(memory_space=pltpu.VMEM)
    return pl.pallas_call(
        core_kernel,
        in_specs=[vmem] * 4,
        out_specs=vmem,
        out_shape=jax.ShapeDtypeStruct((rank, th * ph), jnp.bfloat16),
        scratch_shapes=[pltpu.VMEM((order, order), jnp.float32), pltpu.VMEM((order, rank), jnp.float32)],
        compiler_params=pltpu.CompilerParams(vmem_limit_bytes=VMEM_LIMIT),
        name="subspace_and_core",
    )(mine, other, start, regrouped)


def on_device(field, start):
    radii, th, ph = field.shape
    owners = group(RAD)
    sent = field.transpose(1, 0, 2).reshape(owners, th // owners, radii, ph)
    regrouped = swap(sent, RAD)
    mine, other = sum_everywhere(*partial_gram(regrouped))
    core = core_of(mine, other, start, regrouped)
    return core.reshape(start.shape[1], th // owners, ph)


def solution(mesh):
    fine = Mesh(mesh.devices.reshape(SIZES), AXES)
    return jax.shard_map(
        on_device,
        mesh=fine,
        in_specs=(P(RAD, ("z", "core"), None), P()),
        out_specs=P(None, ("z", "core") + RAD, None),
        check_vma=False,
    )
```

```python
import jax
import jax.numpy as jnp
from jax import lax
from jax.experimental import pallas as pl
from jax.experimental.pallas import tpu as pltpu
from jax.sharding import Mesh, PartitionSpec as P

ITERS = 2
SUB = 8
TILE = 128
TH_STEP = 16
CELLS = 1024
AXES = ("x", "y", "z", "core")
SIZES = (4, 8, 8, 2)
RAD = ("x", "y")
WIDE = ("x", "z")
MID = ("y",)
VMEM_LIMIT = 52 * 2**20


def group(names):
    size = 1
    for name in names:
        size *= SIZES[AXES.index(name)]
    return size


def halves():
    return (((0, 1), (0, 2), (0, 3)), (0, 1)), (((1, 2), (1, 3), (2, 3)), (2, 3))


def tile_iota():
    return (lax.broadcasted_iota(jnp.int32, (TILE, TILE), d) for d in (0, 1))


def regroup_kernel(field_ref, out_ref, held_ref, moved_ref, sems, out_sems):
    radii, th, _ = field_ref.shape
    rows = radii * TH_STEP
    copies = []
    for n in range(th // TH_STEP):
        part = field_ref.at[:, pl.ds(TH_STEP * n, TH_STEP)]
        copies.append(pltpu.make_async_copy(part, held_ref.at[n], sems.at[n]))
        copies[-1].start()
    to = lax.broadcasted_iota(jnp.int32, (rows, rows), 0)
    source = lax.broadcasted_iota(jnp.int32, (rows, rows), 1)
    moved = jnp.where((to // radii == source % TH_STEP) & (to % radii == source // TH_STEP), 1.0, 0.0)
    moved = moved.astype(jnp.bfloat16)
    results = []
    for n, copy in enumerate(copies):
        copy.wait()
        x = held_ref[n].reshape(rows, held_ref.shape[-1])
        y = jnp.dot(moved, x, preferred_element_type=jnp.float32).astype(jnp.bfloat16)
        moved_ref[n] = y.reshape(TH_STEP, radii, held_ref.shape[-1])
        part = out_ref.at[pl.ds(TH_STEP * n, TH_STEP)]
        results.append(pltpu.make_async_copy(moved_ref.at[n], part, out_sems.at[n]))
        results[-1].start()
    for result in results:
        result.wait()


def by_colatitude(field):
    radii, th, ph = field.shape
    parts = th // TH_STEP
    return pl.pallas_call(
        regroup_kernel,
        in_specs=[pl.BlockSpec(memory_space=pltpu.HBM)],
        out_specs=pl.BlockSpec(memory_space=pltpu.HBM),
        out_shape=jax.ShapeDtypeStruct((th, radii, ph), field.dtype),
        scratch_shapes=[
            pltpu.VMEM((parts, radii, TH_STEP, ph), field.dtype),
            pltpu.VMEM((parts, TH_STEP, radii, ph), field.dtype),
            pltpu.SemaphoreType.DMA((parts,)),
            pltpu.SemaphoreType.DMA((parts,)),
        ],
        compiler_params=pltpu.CompilerParams(vmem_limit_bytes=VMEM_LIMIT),
        name="by_colatitude",
    )(field)


def gram_kernel(u_ref, keep_ref, send_ref, acc_ref, held_ref, sems):
    src, th, radii, ph = u_ref.shape
    order = src * radii
    half = order // 2
    copies = []
    for n in range(th * (ph // CELLS)):
        t, c = divmod(n, ph // CELLS)
        part = u_ref.at[:, t, :, pl.ds(CELLS * c, CELLS)]
        copies.append(pltpu.make_async_copy(part, held_ref.at[n], sems.at[n]))
        copies[-1].start()
    for n, copy in enumerate(copies):
        copy.wait()
        u = held_ref[n].reshape(order, CELLS)
        top = lax.dot_general(u[:half], u, (((1,), (1,)), ((), ())), preferred_element_type=jnp.float32)
        low = lax.dot_general(u[half:], u[half:], (((1,), (1,)), ((), ())), preferred_element_type=jnp.float32)
        if n == 0:
            acc_ref[:half] = top
            acc_ref[half:, half:] = low
        else:
            acc_ref[:half] += top
            acc_ref[half:, half:] += low
    row, col = tile_iota()

    def block(i, j):
        return acc_ref[TILE * i:TILE * (i + 1), TILE * j:TILE * (j + 1)]

    def pack(ref, part):
        offs, (first, second) = part
        for n, (i, j) in enumerate(offs):
            ref[TILE * n:TILE * (n + 1)] = block(i, j)
        under = block(first, first)
        ref[TILE * 3:TILE * 4] = jnp.where(row > col, under, block(second, second))
        diagonal = jnp.sum(jnp.where(row == col, under, 0.0), axis=0, keepdims=True)
        ref[TILE * 4:] = jnp.broadcast_to(diagonal, (ref.shape[0] - TILE * 4, TILE))

    core = lax.axis_index("core")
    for own in (0, 1):
        @pl.when(core == own)
        def _():
            pack(keep_ref, halves()[own])
            pack(send_ref, halves()[1 - own])


def partial_gram(regrouped):
    src, th, radii, ph = regrouped.shape
    order = src * radii
    parts = th * (ph // CELLS)
    vmem = pl.BlockSpec(memory_space=pltpu.VMEM)
    out = jax.ShapeDtypeStruct((4 * TILE + group(WIDE), TILE), jnp.float32)
    return pl.pallas_call(
        gram_kernel,
        in_specs=[pl.BlockSpec(memory_space=pltpu.HBM)],
        out_specs=[vmem, vmem],
        out_shape=[out, out],
        scratch_shapes=[
            pltpu.VMEM((order, order), jnp.float32),
            pltpu.VMEM((parts, src, radii, CELLS), jnp.bfloat16),
            pltpu.SemaphoreType.DMA((parts,)),
        ],
        compiler_params=pltpu.CompilerParams(vmem_limit_bytes=VMEM_LIMIT),
        name="gram",
    )(regrouped)


def unpack_half(packed, part, gram_ref):
    offs, (first, second) = part
    row, col = tile_iota()

    def put(i, j, value):
        gram_ref[TILE * i:TILE * (i + 1), TILE * j:TILE * (j + 1)] = value

    for n, (i, j) in enumerate(offs):
        value = packed[TILE * n:TILE * (n + 1)]
        put(i, j, value)
        put(j, i, value.T)
    shared = packed[TILE * 3:TILE * 4]
    diagonal = jnp.broadcast_to(packed[TILE * 4:TILE * 4 + 1], (TILE, TILE))
    turned = shared.T
    put(first, first, jnp.where(row > col, shared, jnp.where(row < col, turned, diagonal)))
    put(second, second, jnp.where(row > col, turned, shared))


def swap(x, names):
    return lax.all_to_all(x, names, split_axis=0, concat_axis=0, tiled=True)


def swap_core(x):
    return lax.ppermute(x, "core", [(0, 1), (1, 0)])


def repeat(x, copies):
    return jnp.broadcast_to(x[None], (copies,) + x.shape)


def sum_everywhere(keep, send):
    half = keep + swap_core(send)
    share = jnp.sum(swap(half.reshape(group(WIDE), 1, -1), WIDE), axis=0)
    share = jnp.sum(swap(repeat(share, group(MID)), MID), axis=0)
    mine = swap(repeat(share, group(WIDE)), WIDE).reshape(half.shape)
    return mine, swap_core(mine)


def inverse_lower(inner):
    n = inner.shape[0]
    parts = n // SUB
    row = lax.broadcasted_iota(jnp.int32, (SUB, n), 0)
    col = lax.broadcasted_iota(jnp.int32, (SUB, n), 1)
    left = [inner[SUB * q:SUB * (q + 1)] for q in range(parts)]
    right = [jnp.where(col == row + SUB * q, 1.0, 0.0) for q in range(parts)]

    def spread(x, c):
        return jnp.broadcast_to(x[:, c:c + 1], (SUB, n))

    def pick(x, r):
        return jnp.broadcast_to(x[r:r + 1], (SUB, n))

    for p in range(parts):
        columns = {q: [spread(left[q], SUB * p + j) for j in range(SUB)] for q in range(p, parts)}
        pivots = jnp.ones((SUB, n), jnp.float32)
        for j in range(SUB):
            own = columns[p]
            pivot = pick(own[j], j)
            inv = 1.0 / pivot
            pivots = jnp.where(row == j, pivot, pivots)
            lead_left = pick(left[p], j)
            lead_right = pick(right[p], j)
            lead = [pick(own[c], j) for c in range(j + 1, SUB)]
            for q in range(p, parts):
                times = columns[q][j] * inv
                if q == p:
                    times = jnp.where(row > j, times, 0.0)
                left[q] = left[q] - times * lead_left
                right[q] = right[q] - times * lead_right
                for c in range(j + 1, SUB):
                    columns[q][c] = columns[q][c] - times * lead[c - j - 1]
        right[p] = right[p] / jnp.sqrt(pivots)
    return jnp.concatenate(right, axis=0)


def exact(a, b, dims):
    return lax.dot_general(
        a, b, ((dims[:1], dims[1:]), ((), ())),
        precision=lax.Precision.HIGHEST, preferred_element_type=jnp.float32,
    )


def core_kernel(mine_ref, other_ref, start_ref, u_ref, out_ref, gram_ref, basis_ref, held_ref, sem):
    copy = pltpu.make_async_copy(u_ref, held_ref, sem)
    copy.start()
    core = lax.axis_index("core")
    for own in (0, 1):
        @pl.when(core == own)
        def _():
            unpack_half(mine_ref[...], halves()[own], gram_ref)
            unpack_half(other_ref[...], halves()[1 - own], gram_ref)
    basis_ref[...] = start_ref[...]

    def step(_, carry):
        grown = exact(gram_ref[...], basis_ref[...], (1, 0))
        inner = exact(grown, grown, (0, 0))
        basis_ref[...] = exact(grown, inverse_lower(inner), (1, 1))
        return carry

    lax.fori_loop(0, ITERS, step, 0)
    narrow = basis_ref[...].T.astype(jnp.bfloat16)
    copy.wait()
    src, th, radii, ph = held_ref.shape
    cells = 512
    for t in range(th):
        for c in range(ph // cells):
            u = held_ref[:, t, :, cells * c:cells * (c + 1)].reshape(src * radii, cells)
            core = jnp.dot(narrow, u, preferred_element_type=jnp.float32)
            out_ref[:, t * ph + cells * c:t * ph + cells * (c + 1)] = core.astype(jnp.bfloat16)


def core_of(mine, other, start, regrouped):
    order, rank = start.shape
    src, th, radii, ph = regrouped.shape
    vmem = pl.BlockSpec(memory_space=pltpu.VMEM)
    return pl.pallas_call(
        core_kernel,
        in_specs=[vmem] * 3 + [pl.BlockSpec(memory_space=pltpu.HBM)],
        out_specs=vmem,
        out_shape=jax.ShapeDtypeStruct((rank, th * ph), jnp.bfloat16),
        scratch_shapes=[
            pltpu.VMEM((order, order), jnp.float32),
            pltpu.VMEM((order, rank), jnp.float32),
            pltpu.VMEM(regrouped.shape, jnp.bfloat16),
            pltpu.SemaphoreType.DMA,
        ],
        compiler_params=pltpu.CompilerParams(vmem_limit_bytes=VMEM_LIMIT),
        name="subspace_and_core",
    )(mine, other, start, regrouped)


def on_device(field, start):
    radii, th, ph = field.shape
    owners = group(RAD)
    sent = by_colatitude(field).reshape(owners, th // owners, radii, ph)
    regrouped = swap(sent, RAD)
    mine, other = sum_everywhere(*partial_gram(regrouped))
    core = core_of(mine, other, start, regrouped)
    return core.reshape(start.shape[1], th // owners, ph)


def solution(mesh):
    fine = Mesh(mesh.devices.reshape(SIZES), AXES)
    return jax.shard_map(
        on_device,
        mesh=fine,
        in_specs=(P(RAD, ("z", "core"), None), P()),
        out_specs=P(None, ("z", "core") + RAD, None),
        check_vma=False,
    )
```

```python
import jax
import jax.numpy as jnp
from jax import lax
from jax.experimental import pallas as pl
from jax.experimental.pallas import tpu as pltpu
from jax.sharding import Mesh, PartitionSpec as P

ITERS = 2
SUB = 8
BLOCK = 16
TILE = 128
TH_STEP = 16
CELLS = 1024
AHEAD = 4
AXES = ("x", "y", "z", "core")
SIZES = (4, 8, 8, 2)
RAD = ("x", "y")
WIDE = ("x", "z")
MID = ("y",)
VMEM_LIMIT = 52 * 2**20
GRAM_LIMIT = 46 * 2**20
HELD_ROOM = 2


def group(names):
    size = 1
    for name in names:
        size *= SIZES[AXES.index(name)]
    return size


def halves():
    return (((0, 1), (0, 2), (0, 3)), (0, 1)), (((1, 2), (1, 3), (2, 3)), (2, 3))


def tile_iota():
    return (lax.broadcasted_iota(jnp.int32, (TILE, TILE), d) for d in (0, 1))


def regroup_kernel(field_ref, out_ref, held_ref, moved_ref, sems, out_sems):
    radii, th, _ = field_ref.shape
    rows = radii * TH_STEP
    copies = []
    for n in range(th // TH_STEP):
        part = field_ref.at[:, pl.ds(TH_STEP * n, TH_STEP)]
        copies.append(pltpu.make_async_copy(part, held_ref.at[n], sems.at[n]))
    for copy in copies[:AHEAD]:
        copy.start()
    to = lax.broadcasted_iota(jnp.int32, (rows, rows), 0)
    source = lax.broadcasted_iota(jnp.int32, (rows, rows), 1)
    moved = jnp.where((to // radii == source % TH_STEP) & (to % radii == source // TH_STEP), 1.0, 0.0)
    moved = moved.astype(jnp.bfloat16)
    results = []
    for n, copy in enumerate(copies):
        copy.wait()
        for later in copies[n + AHEAD:n + AHEAD + 1]:
            later.start()
        x = held_ref[n].reshape(rows, held_ref.shape[-1])
        y = jnp.dot(moved, x, preferred_element_type=jnp.float32).astype(jnp.bfloat16)
        moved_ref[n] = y.reshape(TH_STEP, radii, held_ref.shape[-1])
        part = out_ref.at[pl.ds(TH_STEP * n, TH_STEP)]
        results.append(pltpu.make_async_copy(moved_ref.at[n], part, out_sems.at[n]))
        results[-1].start()
    for result in results:
        result.wait()


def by_colatitude(field):
    radii, th, ph = field.shape
    parts = th // TH_STEP
    return pl.pallas_call(
        regroup_kernel,
        in_specs=[pl.BlockSpec(memory_space=pltpu.HBM)],
        out_specs=pl.BlockSpec(memory_space=pltpu.HBM),
        out_shape=jax.ShapeDtypeStruct((th, radii, ph), field.dtype),
        scratch_shapes=[
            pltpu.VMEM((parts, radii, TH_STEP, ph), field.dtype),
            pltpu.VMEM((parts, TH_STEP, radii, ph), field.dtype),
            pltpu.SemaphoreType.DMA((parts,)),
            pltpu.SemaphoreType.DMA((parts,)),
        ],
        compiler_params=pltpu.CompilerParams(vmem_limit_bytes=VMEM_LIMIT),
        name="by_colatitude",
    )(field)


def gram_kernel(u_ref, keep_ref, send_ref, held_ref, acc_ref, sem):
    src, th, radii, ph = u_ref.shape
    copy = pltpu.make_async_copy(u_ref, held_ref.at[pl.ds(0, src)], sem)
    copy.start()
    order = src * radii
    half = order // 2
    for n in range(th * (ph // CELLS)):
        t, c = divmod(n, ph // CELLS)
        u = u_ref[:, t, :, CELLS * c:CELLS * (c + 1)].reshape(order, CELLS)
        top = lax.dot_general(u[:half], u, (((1,), (1,)), ((), ())), preferred_element_type=jnp.float32)
        low = lax.dot_general(u[half:], u[half:], (((1,), (1,)), ((), ())), preferred_element_type=jnp.float32)
        if n == 0:
            acc_ref[:half] = top
            acc_ref[half:, half:] = low
        else:
            acc_ref[:half] += top
            acc_ref[half:, half:] += low
    row, col = tile_iota()

    def block(i, j):
        return acc_ref[TILE * i:TILE * (i + 1), TILE * j:TILE * (j + 1)]

    def pack(ref, part):
        offs, (first, second) = part
        for n, (i, j) in enumerate(offs):
            ref[TILE * n:TILE * (n + 1)] = block(i, j)
        under = block(first, first)
        ref[TILE * 3:TILE * 4] = jnp.where(row > col, under, block(second, second))
        diagonal = jnp.sum(jnp.where(row == col, under, 0.0), axis=0, keepdims=True)
        ref[TILE * 4:] = jnp.broadcast_to(diagonal, (ref.shape[0] - TILE * 4, TILE))

    core = lax.axis_index("core")
    for own in (0, 1):
        @pl.when(core == own)
        def _():
            pack(keep_ref, halves()[own])
            pack(send_ref, halves()[1 - own])

    copy.wait()


def partial_gram(regrouped):
    src, th, radii, ph = regrouped.shape
    order = src * radii
    vmem = pl.BlockSpec(memory_space=pltpu.VMEM)
    out = jax.ShapeDtypeStruct((4 * TILE + group(WIDE), TILE), jnp.float32)
    return pl.pallas_call(
        gram_kernel,
        in_specs=[vmem],
        out_specs=[vmem, vmem, pl.BlockSpec(memory_space=pltpu.HBM)],
        out_shape=[out, out, jax.ShapeDtypeStruct((HELD_ROOM * src, th, radii, ph), regrouped.dtype)],
        scratch_shapes=[pltpu.VMEM((order, order), jnp.float32), pltpu.SemaphoreType.DMA],
        compiler_params=pltpu.CompilerParams(vmem_limit_bytes=GRAM_LIMIT),
        name="gram",
    )(regrouped)


def unpack_half(packed, part, gram_ref):
    offs, (first, second) = part
    row, col = tile_iota()

    def put(i, j, value):
        gram_ref[TILE * i:TILE * (i + 1), TILE * j:TILE * (j + 1)] = value

    for n, (i, j) in enumerate(offs):
        value = packed[TILE * n:TILE * (n + 1)]
        put(i, j, value)
        put(j, i, value.T)
    shared = packed[TILE * 3:TILE * 4]
    diagonal = jnp.broadcast_to(packed[TILE * 4:TILE * 4 + 1], (TILE, TILE))
    turned = shared.T
    put(first, first, jnp.where(row > col, shared, jnp.where(row < col, turned, diagonal)))
    put(second, second, jnp.where(row > col, turned, shared))


def swap(x, names):
    return lax.all_to_all(x, names, split_axis=0, concat_axis=0, tiled=True)


def swap_core(x):
    return lax.ppermute(x, "core", [(0, 1), (1, 0)])


def repeat(x, copies):
    return jnp.broadcast_to(x[None], (copies,) + x.shape)


def sum_everywhere(keep, send):
    half = keep + swap_core(send)
    share = jnp.sum(swap(half.reshape(group(WIDE), 1, -1), WIDE), axis=0)
    share = jnp.sum(swap(repeat(share, group(MID)), MID), axis=0)
    mine = swap(repeat(share, group(WIDE)), WIDE).reshape(half.shape)
    return mine, swap_core(mine)


def split(x):
    one = x.astype(jnp.bfloat16)
    rest = x - one.astype(jnp.float32)
    two = rest.astype(jnp.bfloat16)
    return one, two, (rest - two.astype(jnp.float32)).astype(jnp.bfloat16)


def outer(a, b):
    a1, a2, a3 = split(a)
    b1, b2, b3 = split(b)
    return lax.dot_general(
        jnp.concatenate([a1, a1, a2, a2, a1, a3], axis=0),
        jnp.concatenate([b1, b2, b1, b2, b3, b1], axis=0),
        (((0,), (0,)), ((), ())), preferred_element_type=jnp.float32,
    )


def inverse_lower(inner):
    n = inner.shape[0]
    row = lax.broadcasted_iota(jnp.int32, (SUB, n), 0)
    col = lax.broadcasted_iota(jnp.int32, (SUB, n), 1)

    def spread(x, c):
        return jnp.broadcast_to(x[:, c:c + 1], (SUB, n))

    def pick(x, r):
        return jnp.broadcast_to(x[r:r + 1], (SUB, n))

    def panels(x, count):
        return [x[SUB * q:SUB * (q + 1)] for q in range(count)]

    done = []
    left_rest, right_rest = inner, jnp.zeros_like(inner)
    for start in range(0, n, BLOCK):
        count = BLOCK // SUB
        left = panels(left_rest, count)
        right = [x + jnp.where(col == row + start + SUB * q, 1.0, 0.0) for q, x in enumerate(panels(right_rest, count))]
        own = [spread(left[0], start + j) for j in range(SUB)]
        scales, roots = [], []
        for p in range(count):
            at = start + SUB * p
            more = p + 1 < count
            if more:
                below = [spread(left[p + 1], at + j) for j in range(SUB)]
                after = [spread(left[p + 1], at + SUB + j) for j in range(SUB)]
            scale = jnp.ones((SUB, n), jnp.float32)
            pivots = jnp.ones((SUB, n), jnp.float32)
            for j in range(SUB):
                pivot = pick(own[j], j)
                inv = 1.0 / pivot
                pivots = jnp.where(row == j, pivot, pivots)
                scale = jnp.where(row == j, inv, scale)
                lead_left, lead_right = pick(left[p], j), pick(right[p], j)
                lead = {c: pick(own[c], j) for c in range(j + 1, SUB)}
                times = jnp.where(row > j, own[j], 0.0) * inv
                for c in range(j + 1, SUB):
                    own[c] = own[c] - times * lead[c]
                left[p] = left[p] - times * lead_left
                right[p] = right[p] - times * lead_right
                if more:
                    times = below[j] * inv
                    for c in range(SUB):
                        after[c] = after[c] - times * pick(below[j], c)
                    for c in range(j + 1, SUB):
                        below[c] = below[c] - times * lead[c]
                    left[p + 1] = left[p + 1] - times * lead_left
                    right[p + 1] = right[p + 1] - times * lead_right
            scales.append(scale)
            roots.append(jnp.sqrt(pivots))
            if more:
                own = after
        left_block = jnp.concatenate(left, axis=0)
        right_block = jnp.concatenate(right, axis=0)
        done.append(right_block / jnp.concatenate(roots, axis=0))
        if start + BLOCK < n:
            scaled = left_block * jnp.concatenate(scales, axis=0)
            change = outer(scaled, jnp.concatenate([left_block, right_block], axis=1))[start + BLOCK:]
            left_rest = left_rest[BLOCK:] - change[:, :n]
            right_rest = right_rest[BLOCK:] - change[:, n:]
    return jnp.concatenate(done, axis=0)


def exact(a, b, dims):
    return lax.dot_general(
        a, b, ((dims[:1], dims[1:]), ((), ())),
        precision=lax.Precision.HIGHEST, preferred_element_type=jnp.float32,
    )


def core_kernel(mine_ref, other_ref, start_ref, u_ref, out_ref, gram_ref, basis_ref, held_ref, sem):
    copy = pltpu.make_async_copy(u_ref.at[pl.ds(0, held_ref.shape[0])], held_ref, sem)
    copy.start()
    core = lax.axis_index("core")
    for own in (0, 1):
        @pl.when(core == own)
        def _():
            unpack_half(mine_ref[...], halves()[own], gram_ref)
            unpack_half(other_ref[...], halves()[1 - own], gram_ref)
    basis_ref[...] = start_ref[...].T

    def step(_, carry):
        grown = exact(basis_ref[...], gram_ref[...], (1, 0))
        inner = exact(grown, grown, (1, 1))
        basis_ref[...] = exact(inverse_lower(inner), grown, (1, 0))
        return carry

    lax.fori_loop(0, ITERS, step, 0)
    narrow = basis_ref[...].astype(jnp.bfloat16)
    copy.wait()
    src, th, radii, ph = held_ref.shape
    cells = 512
    for t in range(th):
        for c in range(ph // cells):
            u = held_ref[:, t, :, cells * c:cells * (c + 1)].reshape(src * radii, cells)
            core = jnp.dot(narrow, u, preferred_element_type=jnp.float32)
            out_ref[:, t * ph + cells * c:t * ph + cells * (c + 1)] = core.astype(jnp.bfloat16)


def core_of(mine, other, start, held):
    order, rank = start.shape
    src, th, radii, ph = held.shape
    src //= HELD_ROOM
    vmem = pl.BlockSpec(memory_space=pltpu.VMEM)
    return pl.pallas_call(
        core_kernel,
        in_specs=[vmem] * 3 + [pl.BlockSpec(memory_space=pltpu.HBM)],
        out_specs=vmem,
        out_shape=jax.ShapeDtypeStruct((rank, th * ph), jnp.bfloat16),
        scratch_shapes=[
            pltpu.VMEM((order, order), jnp.float32),
            pltpu.VMEM((rank, order), jnp.float32),
            pltpu.VMEM((src, th, radii, ph), jnp.bfloat16),
            pltpu.SemaphoreType.DMA,
        ],
        compiler_params=pltpu.CompilerParams(vmem_limit_bytes=VMEM_LIMIT),
        name="subspace_and_core",
    )(mine, other, start, held)


def on_device(field, start):
    radii, th, ph = field.shape
    owners = group(RAD)
    sent = by_colatitude(field).reshape(owners, th // owners, radii, ph)
    regrouped = swap(sent, RAD)
    keep, send, held = partial_gram(regrouped)
    mine, other = sum_everywhere(keep, send)
    core = core_of(mine, other, start, held)
    return core.reshape(start.shape[1], th // owners, ph)


def solution(mesh):
    fine = Mesh(mesh.devices.reshape(SIZES), AXES)
    return jax.shard_map(
        on_device,
        mesh=fine,
        in_specs=(P(RAD, ("z", "core"), None), P()),
        out_specs=P(None, ("z", "core") + RAD, None),
        check_vma=False,
    )
```

```python
import jax
import jax.numpy as jnp
from jax import lax
from jax.experimental import pallas as pl
from jax.experimental.pallas import tpu as pltpu
from jax.sharding import Mesh, PartitionSpec as P

ITERS = 2
SUB = 8
TILE = 128
TH_STEP = 16
PH_STEP = 2048
CELLS = 1024
OUT_CELLS = 1024
AXES = ("x", "y", "z", "core")
SIZES = (4, 8, 8, 2)
RAD = ("x", "y")
WIDE = ("x", "z")
MID = ("y",)
VMEM_LIMIT = 52 * 2**20
GRAM_LIMIT = 46 * 2**20
HELD_ROOM = 2


def group(names):
    size = 1
    for name in names:
        size *= SIZES[AXES.index(name)]
    return size


def halves():
    return (((0, 1), (0, 2), (0, 3)), (0, 1)), (((1, 2), (1, 3), (2, 3)), (2, 3))


def tile_iota():
    return (lax.broadcasted_iota(jnp.int32, (TILE, TILE), d) for d in (0, 1))


def regroup_kernel(field_ref, out_ref, held_ref, moved_ref, sems, out_sems):
    radii, th, ph = field_ref.shape
    rows = radii * TH_STEP
    places = [(t, c) for t in range(0, th, TH_STEP) for c in range(0, ph, PH_STEP)]
    copies, results = [], []
    for n, (t, c) in enumerate(places):
        part = field_ref.at[:, pl.ds(t, TH_STEP), pl.ds(c, PH_STEP)]
        copies.append(pltpu.make_async_copy(part, held_ref.at[n], sems.at[n]))
        copies[-1].start()
    to = lax.broadcasted_iota(jnp.int32, (rows, rows), 0)
    source = lax.broadcasted_iota(jnp.int32, (rows, rows), 1)
    moved = jnp.where((to // radii == source % TH_STEP) & (to % radii == source // TH_STEP), 1.0, 0.0)
    moved = moved.astype(jnp.bfloat16)
    for n, (t, c) in enumerate(places):
        copies[n].wait()
        x = held_ref[n].reshape(rows, PH_STEP)
        y = jnp.dot(moved, x, preferred_element_type=jnp.float32).astype(jnp.bfloat16)
        moved_ref[n] = y.reshape(TH_STEP, radii, PH_STEP)
        part = out_ref.at[pl.ds(t, TH_STEP), :, pl.ds(c, PH_STEP)]
        results.append(pltpu.make_async_copy(moved_ref.at[n], part, out_sems.at[n]))
        results[-1].start()
    for result in results:
        result.wait()


def by_colatitude(field):
    radii, th, ph = field.shape
    parts = (th // TH_STEP) * (ph // PH_STEP)
    return pl.pallas_call(
        regroup_kernel,
        in_specs=[pl.BlockSpec(memory_space=pltpu.HBM)],
        out_specs=pl.BlockSpec(memory_space=pltpu.HBM),
        out_shape=jax.ShapeDtypeStruct((th, radii, ph), field.dtype),
        scratch_shapes=[
            pltpu.VMEM((parts, radii, TH_STEP, PH_STEP), field.dtype),
            pltpu.VMEM((parts, TH_STEP, radii, PH_STEP), field.dtype),
            pltpu.SemaphoreType.DMA((parts,)),
            pltpu.SemaphoreType.DMA((parts,)),
        ],
        compiler_params=pltpu.CompilerParams(vmem_limit_bytes=VMEM_LIMIT),
        name="by_colatitude",
    )(field)


def gram_kernel(u_ref, keep_ref, send_ref, held_ref, acc_ref, sem):
    src, th, radii, ph = u_ref.shape
    copy = pltpu.make_async_copy(u_ref, held_ref.at[pl.ds(0, src)], sem)
    copy.start()
    order = src * radii
    half = order // 2
    for n in range(th * (ph // CELLS)):
        t, c = divmod(n, ph // CELLS)
        u = u_ref[:, t, :, CELLS * c:CELLS * (c + 1)].reshape(order, CELLS)
        top = lax.dot_general(u[:half], u, (((1,), (1,)), ((), ())), preferred_element_type=jnp.float32)
        low = lax.dot_general(u[half:], u[half:], (((1,), (1,)), ((), ())), preferred_element_type=jnp.float32)
        if n == 0:
            acc_ref[:half] = top
            acc_ref[half:, half:] = low
        else:
            acc_ref[:half] += top
            acc_ref[half:, half:] += low
    row, col = tile_iota()

    def block(i, j):
        return acc_ref[TILE * i:TILE * (i + 1), TILE * j:TILE * (j + 1)]

    def pack(ref, part):
        offs, (first, second) = part
        for n, (i, j) in enumerate(offs):
            ref[TILE * n:TILE * (n + 1)] = block(i, j)
        under = block(first, first)
        ref[TILE * 3:TILE * 4] = jnp.where(row > col, under, block(second, second))
        diagonal = jnp.sum(jnp.where(row == col, under, 0.0), axis=0, keepdims=True)
        ref[TILE * 4:] = jnp.broadcast_to(diagonal, (ref.shape[0] - TILE * 4, TILE))

    core = lax.axis_index("core")
    for own in (0, 1):
        @pl.when(core == own)
        def _():
            pack(keep_ref, halves()[own])
            pack(send_ref, halves()[1 - own])

    copy.wait()


def partial_gram(regrouped):
    src, th, radii, ph = regrouped.shape
    order = src * radii
    vmem = pl.BlockSpec(memory_space=pltpu.VMEM)
    out = jax.ShapeDtypeStruct((4 * TILE + group(WIDE), TILE), jnp.float32)
    return pl.pallas_call(
        gram_kernel,
        in_specs=[vmem],
        out_specs=[vmem, vmem, pl.BlockSpec(memory_space=pltpu.HBM)],
        out_shape=[out, out, jax.ShapeDtypeStruct((HELD_ROOM * src, th, radii, ph), regrouped.dtype)],
        scratch_shapes=[pltpu.VMEM((order, order), jnp.float32), pltpu.SemaphoreType.DMA],
        compiler_params=pltpu.CompilerParams(vmem_limit_bytes=GRAM_LIMIT),
        name="gram",
    )(regrouped)


def unpack_half(packed, part, gram_ref):
    offs, (first, second) = part
    row, col = tile_iota()

    def put(i, j, value):
        gram_ref[TILE * i:TILE * (i + 1), TILE * j:TILE * (j + 1)] = value

    for n, (i, j) in enumerate(offs):
        value = packed[TILE * n:TILE * (n + 1)]
        put(i, j, value)
        put(j, i, value.T)
    shared = packed[TILE * 3:TILE * 4]
    diagonal = jnp.broadcast_to(packed[TILE * 4:TILE * 4 + 1], (TILE, TILE))
    turned = shared.T
    put(first, first, jnp.where(row > col, shared, jnp.where(row < col, turned, diagonal)))
    put(second, second, jnp.where(row > col, turned, shared))


def swap(x, names):
    return lax.all_to_all(x, names, split_axis=0, concat_axis=0, tiled=True)


def swap_core(x):
    return lax.ppermute(x, "core", [(0, 1), (1, 0)])


def repeat(x, copies):
    return jnp.broadcast_to(x[None], (copies,) + x.shape)


def sum_everywhere(keep, send):
    half = keep + swap_core(send)
    share = jnp.sum(swap(half.reshape(group(WIDE), 1, -1), WIDE), axis=0)
    share = jnp.sum(swap(repeat(share, group(MID)), MID), axis=0)
    mine = swap(repeat(share, group(WIDE)), WIDE).reshape(half.shape)
    return mine, swap_core(mine)


def split(x):
    one = x.astype(jnp.bfloat16)
    rest = x - one.astype(jnp.float32)
    two = rest.astype(jnp.bfloat16)
    return one, two, (rest - two.astype(jnp.float32)).astype(jnp.bfloat16)


def outer(a, b):
    a1, a2, a3 = split(a)
    b1, b2, b3 = split(b)
    return lax.dot_general(
        jnp.concatenate([a1, a1, a2, a2, a1, a3], axis=0),
        jnp.concatenate([b1, b2, b1, b2, b3, b1], axis=0),
        (((0,), (0,)), ((), ())), preferred_element_type=jnp.float32,
    )


def inverse_lower(inner):
    n = inner.shape[0]
    parts = n // SUB
    row = lax.broadcasted_iota(jnp.int32, (SUB, n), 0)
    col = lax.broadcasted_iota(jnp.int32, (SUB, n), 1)

    def spread(x, c):
        return jnp.broadcast_to(x[:, c:c + 1], (SUB, n))

    def pick(x, r):
        return jnp.broadcast_to(x[r:r + 1], (SUB, n))

    rows = [inner[SUB * q:SUB * (q + 1)] for q in range(parts)]
    own = [spread(rows[0], j) for j in range(SUB)]
    done = []
    for p in range(parts):
        at = SUB * p
        more = p + 1 < parts
        inside = (col >= at) & (col < at + SUB)
        if more:
            below = [spread(rows[p + 1], at + j) for j in range(SUB)]
            after = [spread(rows[p + 1], at + SUB + j) for j in range(SUB)]
            rows[p + 1] = jnp.where(inside, 0.0, rows[p + 1])
        rows[p] = jnp.where(inside, jnp.where(col == row + at, 1.0, 0.0), rows[p])
        scale = jnp.ones((SUB, n), jnp.float32)
        pivots = jnp.ones((SUB, n), jnp.float32)
        for j in range(SUB):
            pivot = pick(own[j], j)
            inv = 1.0 / pivot
            pivots = jnp.where(row == j, pivot, pivots)
            scale = jnp.where(row == j, inv, scale)
            lead_row = pick(rows[p], j)
            lead = {c: pick(own[c], j) for c in range(j + 1, SUB)}
            times = jnp.where(row > j, own[j], 0.0) * inv
            for c in range(j + 1, SUB):
                own[c] = own[c] - times * lead[c]
            rows[p] = rows[p] - times * lead_row
            if more:
                times = below[j] * inv
                for c in range(SUB):
                    after[c] = after[c] - times * pick(below[j], c)
                for c in range(j + 1, SUB):
                    below[c] = below[c] - times * lead[c]
                rows[p + 1] = rows[p + 1] - times * lead_row
        done.append(rows[p] / jnp.sqrt(pivots))
        if p + 2 < parts:
            change = outer(rows[p] * scale, rows[p])
            for q in range(p + 2, parts):
                rows[q] = jnp.where(inside, 0.0, rows[q]) - change[SUB * q:SUB * (q + 1)]
        if more:
            own = after
    lower = lax.broadcasted_iota(jnp.int32, (n, n), 0) >= lax.broadcasted_iota(jnp.int32, (n, n), 1)
    return jnp.where(lower, jnp.concatenate(done, axis=0), 0.0)


def exact(a, b, dims):
    return lax.dot_general(
        a, b, ((dims[:1], dims[1:]), ((), ())),
        precision=lax.Precision.HIGHEST, preferred_element_type=jnp.float32,
    )


def core_kernel(
    mine_ref, other_ref, start_ref, u_ref, out_ref, gram_ref, basis_ref, held_ref, core_part_ref, sem, out_sems
):
    copy = pltpu.make_async_copy(u_ref.at[pl.ds(0, held_ref.shape[0])], held_ref, sem)
    copy.start()
    core = lax.axis_index("core")
    for own in (0, 1):
        @pl.when(core == own)
        def _():
            unpack_half(mine_ref[...], halves()[own], gram_ref)
            unpack_half(other_ref[...], halves()[1 - own], gram_ref)
    basis_ref[...] = start_ref[...].T

    def step(_, carry):
        grown = exact(basis_ref[...], gram_ref[...], (1, 0))
        inner = exact(grown, grown, (1, 1))
        basis_ref[...] = exact(inverse_lower(inner), grown, (1, 0))
        return carry

    lax.fori_loop(0, ITERS, step, 0)
    narrow = basis_ref[...].astype(jnp.bfloat16)
    copy.wait()
    src, th, radii, ph = held_ref.shape
    results = []
    for c in range(ph // OUT_CELLS):
        cells = slice(OUT_CELLS * c, OUT_CELLS * (c + 1))
        for t in range(th):
            u = held_ref[:, t, :, cells].reshape(src * radii, OUT_CELLS)
            core_part_ref[:, t, cells] = jnp.dot(narrow, u, preferred_element_type=jnp.float32).astype(jnp.bfloat16)
        part = pl.ds(OUT_CELLS * c, OUT_CELLS)
        results.append(pltpu.make_async_copy(core_part_ref.at[:, :, part], out_ref.at[:, :, part], out_sems.at[c]))
        results[-1].start()
    for result in results:
        result.wait()


def core_of(mine, other, start, held):
    order, rank = start.shape
    src, th, radii, ph = held.shape
    src //= HELD_ROOM
    vmem = pl.BlockSpec(memory_space=pltpu.VMEM)
    return pl.pallas_call(
        core_kernel,
        in_specs=[vmem] * 3 + [pl.BlockSpec(memory_space=pltpu.HBM)],
        out_specs=pl.BlockSpec(memory_space=pltpu.HBM),
        out_shape=jax.ShapeDtypeStruct((rank, th, ph), jnp.bfloat16),
        scratch_shapes=[
            pltpu.VMEM((order, order), jnp.float32),
            pltpu.VMEM((rank, order), jnp.float32),
            pltpu.VMEM((src, th, radii, ph), jnp.bfloat16),
            pltpu.VMEM((rank, th, ph), jnp.bfloat16),
            pltpu.SemaphoreType.DMA,
            pltpu.SemaphoreType.DMA((ph // OUT_CELLS,)),
        ],
        compiler_params=pltpu.CompilerParams(vmem_limit_bytes=VMEM_LIMIT),
        name="subspace_and_core",
    )(mine, other, start, held)


def on_device(field, start):
    radii, th, ph = field.shape
    owners = group(RAD)
    sent = by_colatitude(field).reshape(owners, th // owners, radii, ph)
    regrouped = swap(sent, RAD)
    keep, send, held = partial_gram(regrouped)
    mine, other = sum_everywhere(keep, send)
    return core_of(mine, other, start, held)


def solution(mesh):
    fine = Mesh(mesh.devices.reshape(SIZES), AXES)
    return jax.shard_map(
        on_device,
        mesh=fine,
        in_specs=(P(RAD, ("z", "core"), None), P()),
        out_specs=P(None, ("z", "core") + RAD, None),
        check_vma=False,
    )
```

```python
import jax
import jax.numpy as jnp
from jax import lax
from jax.experimental import pallas as pl
from jax.experimental.pallas import tpu as pltpu
from jax.sharding import Mesh, PartitionSpec as P

ITERS = 2
SUB = 8
LOOK = 3
TILE = 128
TH_STEP = 16
CELLS = 1024
OUT_CELLS = 1024
AXES = ("x", "y", "z", "core")
SIZES = (4, 8, 8, 2)
RAD = ("x", "y")
WIDE = ("x", "z")
MID = ("y",)
VMEM_LIMIT = 52 * 2**20
GRAM_LIMIT = 46 * 2**20
REGROUP_LIMIT = 48 * 2**20
HELD_ROOM = 2


def group(names):
    size = 1
    for name in names:
        size *= SIZES[AXES.index(name)]
    return size


def halves():
    return (((0, 1), (0, 2), (0, 3)), (0, 1)), (((1, 2), (1, 3), (2, 3)), (2, 3))


def tile_iota():
    return (lax.broadcasted_iota(jnp.int32, (TILE, TILE), d) for d in (0, 1))


def regroup_kernel(field_ref, out_ref, held_ref, sems):
    radii, th, ph = field_ref.shape
    rows = radii * TH_STEP
    copies = []
    for n in range(th // TH_STEP):
        part = field_ref.at[:, pl.ds(TH_STEP * n, TH_STEP)]
        copies.append(pltpu.make_async_copy(part, held_ref.at[n], sems.at[n]))
        copies[-1].start()
    to = lax.broadcasted_iota(jnp.int32, (rows, rows), 0)
    source = lax.broadcasted_iota(jnp.int32, (rows, rows), 1)
    moved = jnp.where((to // radii == source % TH_STEP) & (to % radii == source // TH_STEP), 1.0, 0.0)
    moved = moved.astype(jnp.bfloat16)
    for n, copy in enumerate(copies):
        copy.wait()
        x = held_ref[n].reshape(rows, ph)
        y = jnp.dot(moved, x, preferred_element_type=jnp.float32).astype(jnp.bfloat16)
        out_ref[TH_STEP * n:TH_STEP * (n + 1)] = y.reshape(TH_STEP, radii, ph)


def by_colatitude(field):
    radii, th, ph = field.shape
    parts = th // TH_STEP
    return pl.pallas_call(
        regroup_kernel,
        in_specs=[pl.BlockSpec(memory_space=pltpu.HBM)],
        out_specs=pl.BlockSpec(memory_space=pltpu.VMEM),
        out_shape=jax.ShapeDtypeStruct((th, radii, ph), field.dtype),
        scratch_shapes=[pltpu.VMEM((parts, radii, TH_STEP, ph), field.dtype), pltpu.SemaphoreType.DMA((parts,))],
        compiler_params=pltpu.CompilerParams(vmem_limit_bytes=REGROUP_LIMIT),
        name="by_colatitude",
    )(field)


def gram_kernel(u_ref, keep_ref, send_ref, held_ref, acc_ref, sem):
    src, th, radii, ph = u_ref.shape
    copy = pltpu.make_async_copy(u_ref, held_ref.at[pl.ds(0, src)], sem)
    copy.start()
    order = src * radii
    half = order // 2
    for n in range(th * (ph // CELLS)):
        t, c = divmod(n, ph // CELLS)
        u = u_ref[:, t, :, CELLS * c:CELLS * (c + 1)].reshape(order, CELLS)
        top = lax.dot_general(u[:half], u, (((1,), (1,)), ((), ())), preferred_element_type=jnp.float32)
        low = lax.dot_general(u[half:], u[half:], (((1,), (1,)), ((), ())), preferred_element_type=jnp.float32)
        if n == 0:
            acc_ref[:half] = top
            acc_ref[half:, half:] = low
        else:
            acc_ref[:half] += top
            acc_ref[half:, half:] += low
    row, col = tile_iota()

    def block(i, j):
        return acc_ref[TILE * i:TILE * (i + 1), TILE * j:TILE * (j + 1)]

    def pack(ref, part):
        offs, (first, second) = part
        for n, (i, j) in enumerate(offs):
            ref[TILE * n:TILE * (n + 1)] = block(i, j)
        under = block(first, first)
        ref[TILE * 3:TILE * 4] = jnp.where(row > col, under, block(second, second))
        diagonal = jnp.sum(jnp.where(row == col, under, 0.0), axis=0, keepdims=True)
        ref[TILE * 4:] = jnp.broadcast_to(diagonal, (ref.shape[0] - TILE * 4, TILE))

    core = lax.axis_index("core")
    for own in (0, 1):
        @pl.when(core == own)
        def _():
            pack(keep_ref, halves()[own])
            pack(send_ref, halves()[1 - own])

    copy.wait()


def partial_gram(regrouped):
    src, th, radii, ph = regrouped.shape
    order = src * radii
    vmem = pl.BlockSpec(memory_space=pltpu.VMEM)
    out = jax.ShapeDtypeStruct((4 * TILE + group(WIDE), TILE), jnp.float32)
    return pl.pallas_call(
        gram_kernel,
        in_specs=[vmem],
        out_specs=[vmem, vmem, pl.BlockSpec(memory_space=pltpu.HBM)],
        out_shape=[out, out, jax.ShapeDtypeStruct((HELD_ROOM * src, th, radii, ph), regrouped.dtype)],
        scratch_shapes=[pltpu.VMEM((order, order), jnp.float32), pltpu.SemaphoreType.DMA],
        compiler_params=pltpu.CompilerParams(vmem_limit_bytes=GRAM_LIMIT),
        name="gram",
    )(regrouped)


def unpack_half(packed, part, gram_ref):
    offs, (first, second) = part
    row, col = tile_iota()

    def put(i, j, value):
        gram_ref[TILE * i:TILE * (i + 1), TILE * j:TILE * (j + 1)] = value

    for n, (i, j) in enumerate(offs):
        value = packed[TILE * n:TILE * (n + 1)]
        put(i, j, value)
        put(j, i, value.T)
    shared = packed[TILE * 3:TILE * 4]
    diagonal = jnp.broadcast_to(packed[TILE * 4:TILE * 4 + 1], (TILE, TILE))
    turned = shared.T
    put(first, first, jnp.where(row > col, shared, jnp.where(row < col, turned, diagonal)))
    put(second, second, jnp.where(row > col, turned, shared))


def swap(x, names):
    return lax.all_to_all(x, names, split_axis=0, concat_axis=0, tiled=True)


def swap_core(x):
    return lax.ppermute(x, "core", [(0, 1), (1, 0)])


def repeat(x, copies):
    return jnp.broadcast_to(x[None], (copies,) + x.shape)


def sum_everywhere(keep, send):
    half = keep + swap_core(send)
    share = jnp.sum(swap(half.reshape(group(WIDE), 1, -1), WIDE), axis=0)
    share = jnp.sum(swap(repeat(share, group(MID)), MID), axis=0)
    mine = swap(repeat(share, group(WIDE)), WIDE).reshape(half.shape)
    return mine, swap_core(mine)


def split(x):
    one = x.astype(jnp.bfloat16)
    rest = x - one.astype(jnp.float32)
    two = rest.astype(jnp.bfloat16)
    return one, two, (rest - two.astype(jnp.float32)).astype(jnp.bfloat16)


def outer(a, b):
    a1, a2, a3 = split(a)
    b1, b2, b3 = split(b)
    return lax.dot_general(
        jnp.concatenate([a1, a1, a2, a2, a1, a3], axis=0),
        jnp.concatenate([b1, b2, b1, b2, b3, b1], axis=0),
        (((0,), (0,)), ((), ())), preferred_element_type=jnp.float32,
    )


def inverse_lower(inner):
    n = inner.shape[0]
    parts = n // SUB
    row = lax.broadcasted_iota(jnp.int32, (SUB, n), 0)
    col = lax.broadcasted_iota(jnp.int32, (SUB, n), 1)

    def spread(x, c):
        return jnp.broadcast_to(x[:, c:c + 1], (SUB, n))

    def pick(x, r):
        return jnp.broadcast_to(x[r:r + 1], (SUB, n))

    rows = [inner[SUB * q:SUB * (q + 1)] for q in range(parts)]
    own = [spread(rows[0], j) for j in range(SUB)]
    done = []
    for p in range(parts):
        at = SUB * p
        near = range(p + 1, min(parts, p + 1 + LOOK))
        inside = (col >= at) & (col < at + SUB)
        below = {q: [spread(rows[q], at + j) for j in range(SUB)] for q in near}
        if near:
            after = [spread(rows[p + 1], at + SUB + j) for j in range(SUB)]
        for q in near:
            rows[q] = jnp.where(inside, 0.0, rows[q])
        rows[p] = jnp.where(inside, jnp.where(col == row + at, 1.0, 0.0), rows[p])
        scale = jnp.ones((SUB, n), jnp.float32)
        pivots = jnp.ones((SUB, n), jnp.float32)
        for j in range(SUB):
            pivot = pick(own[j], j)
            inv = 1.0 / pivot
            pivots = jnp.where(row == j, pivot, pivots)
            scale = jnp.where(row == j, inv, scale)
            lead_row = pick(rows[p], j)
            lead = {c: pick(own[c], j) for c in range(j + 1, SUB)}
            times = jnp.where(row > j, own[j], 0.0) * inv
            for c in range(j + 1, SUB):
                own[c] = own[c] - times * lead[c]
            rows[p] = rows[p] - times * lead_row
            for q in near:
                times = below[q][j] * inv
                if q == p + 1:
                    for c in range(SUB):
                        after[c] = after[c] - times * pick(below[q][j], c)
                for c in range(j + 1, SUB):
                    below[q][c] = below[q][c] - times * lead[c]
                rows[q] = rows[q] - times * lead_row
        done.append(rows[p] / jnp.sqrt(pivots))
        if p + 1 + LOOK < parts:
            change = outer(rows[p] * scale, rows[p])
            for q in range(p + 1 + LOOK, parts):
                rows[q] = jnp.where(inside, 0.0, rows[q]) - change[SUB * q:SUB * (q + 1)]
        if near:
            own = after
    lower = lax.broadcasted_iota(jnp.int32, (n, n), 0) >= lax.broadcasted_iota(jnp.int32, (n, n), 1)
    return jnp.where(lower, jnp.concatenate(done, axis=0), 0.0)


def exact(a, b, dims):
    return lax.dot_general(
        a, b, ((dims[:1], dims[1:]), ((), ())),
        precision=lax.Precision.HIGHEST, preferred_element_type=jnp.float32,
    )


def core_kernel(
    mine_ref, other_ref, start_ref, u_ref, out_ref, gram_ref, basis_ref, held_ref, core_part_ref, sem, out_sems
):
    copy = pltpu.make_async_copy(u_ref.at[pl.ds(0, held_ref.shape[0])], held_ref, sem)
    copy.start()
    core = lax.axis_index("core")
    for own in (0, 1):
        @pl.when(core == own)
        def _():
            unpack_half(mine_ref[...], halves()[own], gram_ref)
            unpack_half(other_ref[...], halves()[1 - own], gram_ref)
    basis_ref[...] = start_ref[...].T

    def step(_, carry):
        grown = exact(basis_ref[...], gram_ref[...], (1, 0))
        inner = exact(grown, grown, (1, 1))
        basis_ref[...] = exact(inverse_lower(inner), grown, (1, 0))
        return carry

    lax.fori_loop(0, ITERS, step, 0)
    narrow = basis_ref[...].astype(jnp.bfloat16)
    copy.wait()
    src, th, radii, ph = held_ref.shape
    results = []
    for c in range(ph // OUT_CELLS):
        cells = slice(OUT_CELLS * c, OUT_CELLS * (c + 1))
        for t in range(th):
            u = held_ref[:, t, :, cells].reshape(src * radii, OUT_CELLS)
            core_part_ref[:, t, cells] = jnp.dot(narrow, u, preferred_element_type=jnp.float32).astype(jnp.bfloat16)
        part = pl.ds(OUT_CELLS * c, OUT_CELLS)
        results.append(pltpu.make_async_copy(core_part_ref.at[:, :, part], out_ref.at[:, :, part], out_sems.at[c]))
        results[-1].start()
    for result in results:
        result.wait()


def core_of(mine, other, start, held):
    order, rank = start.shape
    src, th, radii, ph = held.shape
    src //= HELD_ROOM
    vmem = pl.BlockSpec(memory_space=pltpu.VMEM)
    return pl.pallas_call(
        core_kernel,
        in_specs=[vmem] * 3 + [pl.BlockSpec(memory_space=pltpu.HBM)],
        out_specs=pl.BlockSpec(memory_space=pltpu.HBM),
        out_shape=jax.ShapeDtypeStruct((rank, th, ph), jnp.bfloat16),
        scratch_shapes=[
            pltpu.VMEM((order, order), jnp.float32),
            pltpu.VMEM((rank, order), jnp.float32),
            pltpu.VMEM((src, th, radii, ph), jnp.bfloat16),
            pltpu.VMEM((rank, th, ph), jnp.bfloat16),
            pltpu.SemaphoreType.DMA,
            pltpu.SemaphoreType.DMA((ph // OUT_CELLS,)),
        ],
        compiler_params=pltpu.CompilerParams(vmem_limit_bytes=VMEM_LIMIT),
        name="subspace_and_core",
    )(mine, other, start, held)


def on_device(field, start):
    radii, th, ph = field.shape
    owners = group(RAD)
    sent = by_colatitude(field).reshape(owners, th // owners, radii, ph)
    regrouped = swap(sent, RAD)
    keep, send, held = partial_gram(regrouped)
    mine, other = sum_everywhere(keep, send)
    return core_of(mine, other, start, held)


def solution(mesh):
    fine = Mesh(mesh.devices.reshape(SIZES), AXES)
    return jax.shard_map(
        on_device,
        mesh=fine,
        in_specs=(P(RAD, ("z", "core"), None), P()),
        out_specs=P(None, ("z", "core") + RAD, None),
        check_vma=False,
    )
```

```python
import jax
import jax.numpy as jnp
from jax import lax
from jax.experimental import pallas as pl
from jax.experimental.pallas import tpu as pltpu
from jax.sharding import Mesh, PartitionSpec as P

ITERS = 2
SUB = 8
LOOK = 3
CARRY = 2
TILE = 128
TH_STEP = 16
CELLS = 1024
OUT_CELLS = 1024
AXES = ("x", "y", "z", "core")
SIZES = (4, 8, 8, 2)
RAD = ("x", "y")
WIDE = ("x", "z")
MID = ("y",)
VMEM_LIMIT = 52 * 2**20
GRAM_LIMIT = 46 * 2**20
REGROUP_LIMIT = 48 * 2**20
HELD_ROOM = 2


def group(names):
    size = 1
    for name in names:
        size *= SIZES[AXES.index(name)]
    return size


def halves():
    return (((0, 1), (0, 2), (0, 3)), (0, 1)), (((1, 2), (1, 3), (2, 3)), (2, 3))


def tile_iota():
    return (lax.broadcasted_iota(jnp.int32, (TILE, TILE), d) for d in (0, 1))


def regroup_kernel(field_ref, out_ref, held_ref, sems):
    radii, th, ph = field_ref.shape
    rows = radii * TH_STEP
    copies = []
    for n in range(th // TH_STEP):
        part = field_ref.at[:, pl.ds(TH_STEP * n, TH_STEP)]
        copies.append(pltpu.make_async_copy(part, held_ref.at[n], sems.at[n]))
        copies[-1].start()
    to = lax.broadcasted_iota(jnp.int32, (rows, rows), 0)
    source = lax.broadcasted_iota(jnp.int32, (rows, rows), 1)
    moved = jnp.where((to // radii == source % TH_STEP) & (to % radii == source // TH_STEP), 1.0, 0.0)
    moved = moved.astype(jnp.bfloat16)
    for n, copy in enumerate(copies):
        copy.wait()
        x = held_ref[n].reshape(rows, ph)
        y = jnp.dot(moved, x, preferred_element_type=jnp.float32).astype(jnp.bfloat16)
        out_ref[TH_STEP * n:TH_STEP * (n + 1)] = y.reshape(TH_STEP, radii, ph)


def by_colatitude(field):
    radii, th, ph = field.shape
    parts = th // TH_STEP
    return pl.pallas_call(
        regroup_kernel,
        in_specs=[pl.BlockSpec(memory_space=pltpu.HBM)],
        out_specs=pl.BlockSpec(memory_space=pltpu.VMEM),
        out_shape=jax.ShapeDtypeStruct((th, radii, ph), field.dtype),
        scratch_shapes=[pltpu.VMEM((parts, radii, TH_STEP, ph), field.dtype), pltpu.SemaphoreType.DMA((parts,))],
        compiler_params=pltpu.CompilerParams(vmem_limit_bytes=REGROUP_LIMIT),
        name="by_colatitude",
    )(field)


def gram_kernel(u_ref, keep_ref, send_ref, held_ref, acc_ref, sem):
    src, th, radii, ph = u_ref.shape
    copy = pltpu.make_async_copy(u_ref, held_ref.at[pl.ds(0, src)], sem)
    copy.start()
    order = src * radii
    half = order // 2
    for n in range(th * (ph // CELLS)):
        t, c = divmod(n, ph // CELLS)
        u = u_ref[:, t, :, CELLS * c:CELLS * (c + 1)].reshape(order, CELLS)
        top = lax.dot_general(u[:half], u, (((1,), (1,)), ((), ())), preferred_element_type=jnp.float32)
        low = lax.dot_general(u[half:], u[half:], (((1,), (1,)), ((), ())), preferred_element_type=jnp.float32)
        if n == 0:
            acc_ref[:half] = top
            acc_ref[half:, half:] = low
        else:
            acc_ref[:half] += top
            acc_ref[half:, half:] += low
    row, col = tile_iota()

    def block(i, j):
        return acc_ref[TILE * i:TILE * (i + 1), TILE * j:TILE * (j + 1)]

    def pack(ref, part):
        offs, (first, second) = part
        for n, (i, j) in enumerate(offs):
            ref[TILE * n:TILE * (n + 1)] = block(i, j)
        under = block(first, first)
        ref[TILE * 3:TILE * 4] = jnp.where(row > col, under, block(second, second))
        diagonal = jnp.sum(jnp.where(row == col, under, 0.0), axis=0, keepdims=True)
        ref[TILE * 4:] = jnp.broadcast_to(diagonal, (ref.shape[0] - TILE * 4, TILE))

    core = lax.axis_index("core")
    for own in (0, 1):
        @pl.when(core == own)
        def _():
            pack(keep_ref, halves()[own])
            pack(send_ref, halves()[1 - own])

    copy.wait()


def partial_gram(regrouped):
    src, th, radii, ph = regrouped.shape
    order = src * radii
    vmem = pl.BlockSpec(memory_space=pltpu.VMEM)
    out = jax.ShapeDtypeStruct((4 * TILE + group(WIDE), TILE), jnp.float32)
    return pl.pallas_call(
        gram_kernel,
        in_specs=[vmem],
        out_specs=[vmem, vmem, pl.BlockSpec(memory_space=pltpu.HBM)],
        out_shape=[out, out, jax.ShapeDtypeStruct((HELD_ROOM * src, th, radii, ph), regrouped.dtype)],
        scratch_shapes=[pltpu.VMEM((order, order), jnp.float32), pltpu.SemaphoreType.DMA],
        compiler_params=pltpu.CompilerParams(vmem_limit_bytes=GRAM_LIMIT),
        name="gram",
    )(regrouped)


def unpack_half(packed, part, gram_ref):
    offs, (first, second) = part
    row, col = tile_iota()

    def put(i, j, value):
        gram_ref[TILE * i:TILE * (i + 1), TILE * j:TILE * (j + 1)] = value

    for n, (i, j) in enumerate(offs):
        value = packed[TILE * n:TILE * (n + 1)]
        put(i, j, value)
        put(j, i, value.T)
    shared = packed[TILE * 3:TILE * 4]
    diagonal = jnp.broadcast_to(packed[TILE * 4:TILE * 4 + 1], (TILE, TILE))
    turned = shared.T
    put(first, first, jnp.where(row > col, shared, jnp.where(row < col, turned, diagonal)))
    put(second, second, jnp.where(row > col, turned, shared))


def swap(x, names):
    return lax.all_to_all(x, names, split_axis=0, concat_axis=0, tiled=True)


def swap_core(x):
    return lax.ppermute(x, "core", [(0, 1), (1, 0)])


def repeat(x, copies):
    return jnp.broadcast_to(x[None], (copies,) + x.shape)


def sum_everywhere(keep, send):
    half = keep + swap_core(send)
    share = jnp.sum(swap(half.reshape(group(WIDE), 1, -1), WIDE), axis=0)
    share = jnp.sum(swap(repeat(share, group(MID)), MID), axis=0)
    mine = swap(repeat(share, group(WIDE)), WIDE).reshape(half.shape)
    return mine, swap_core(mine)


def split(x):
    one = x.astype(jnp.bfloat16)
    rest = x - one.astype(jnp.float32)
    two = rest.astype(jnp.bfloat16)
    return one, two, (rest - two.astype(jnp.float32)).astype(jnp.bfloat16)


def outer(a, b):
    a1, a2, a3 = split(a)
    b1, b2, b3 = split(b)
    return lax.dot_general(
        jnp.concatenate([a1, a1, a2, a2, a1, a3], axis=0),
        jnp.concatenate([b1, b2, b1, b2, b3, b1], axis=0),
        (((0,), (0,)), ((), ())), preferred_element_type=jnp.float32,
    )


def inverse_lower(inner):
    n = inner.shape[0]
    parts = n // SUB
    row = lax.broadcasted_iota(jnp.int32, (SUB, n), 0)
    col = lax.broadcasted_iota(jnp.int32, (SUB, n), 1)

    def spread(x, c):
        return jnp.broadcast_to(x[:, c:c + 1], (SUB, n))

    def pick(x, r):
        return jnp.broadcast_to(x[r:r + 1], (SUB, n))

    rows = [inner[SUB * q:SUB * (q + 1)] for q in range(parts)]
    own = [spread(rows[0], j) for j in range(SUB)]
    below = {}
    done = []
    for p in range(parts):
        at = SUB * p
        near = range(p + 1, min(parts, p + 1 + LOOK))
        inside = (col >= at) & (col < at + SUB)
        for q in near:
            if q not in below:
                below[q] = [spread(rows[q], at + j) for j in range(SUB)]
        after = {q: [spread(rows[q], at + SUB + j) for j in range(SUB)] for q in near if q <= p + CARRY}
        for q in near:
            rows[q] = jnp.where(inside, 0.0, rows[q])
        rows[p] = jnp.where(inside, jnp.where(col == row + at, 1.0, 0.0), rows[p])
        scale = jnp.ones((SUB, n), jnp.float32)
        pivots = jnp.ones((SUB, n), jnp.float32)
        for j in range(SUB):
            pivot = pick(own[j], j)
            inv = 1.0 / pivot
            pivots = jnp.where(row == j, pivot, pivots)
            scale = jnp.where(row == j, inv, scale)
            lead_row = pick(rows[p], j)
            lead = {c: pick(own[c], j) for c in range(j + 1, SUB)}
            times = jnp.where(row > j, own[j], 0.0) * inv
            for c in range(j + 1, SUB):
                own[c] = own[c] - times * lead[c]
            rows[p] = rows[p] - times * lead_row
            if near:
                ahead = [pick(below[p + 1][j], c) for c in range(SUB)]
            for q in near:
                times = below[q][j] * inv
                if q in after:
                    after[q] = [x - times * y for x, y in zip(after[q], ahead)]
                for c in range(j + 1, SUB):
                    below[q][c] = below[q][c] - times * lead[c]
                rows[q] = rows[q] - times * lead_row
        done.append(rows[p] / jnp.sqrt(pivots))
        if p + 1 + LOOK < parts:
            change = outer(rows[p] * scale, rows[p])
            for q in range(p + 1 + LOOK, parts):
                rows[q] = jnp.where(inside, 0.0, rows[q]) - change[SUB * q:SUB * (q + 1)]
        if near:
            own = after.pop(p + 1)
            below = after
    lower = lax.broadcasted_iota(jnp.int32, (n, n), 0) >= lax.broadcasted_iota(jnp.int32, (n, n), 1)
    return jnp.where(lower, jnp.concatenate(done, axis=0), 0.0)


def exact(a, b, dims):
    return lax.dot_general(
        a, b, ((dims[:1], dims[1:]), ((), ())),
        precision=lax.Precision.HIGHEST, preferred_element_type=jnp.float32,
    )


def core_kernel(
    mine_ref, other_ref, start_ref, u_ref, out_ref, gram_ref, basis_ref, held_ref, core_part_ref, sem, out_sems
):
    copy = pltpu.make_async_copy(u_ref.at[pl.ds(0, held_ref.shape[0])], held_ref, sem)
    copy.start()
    core = lax.axis_index("core")
    for own in (0, 1):
        @pl.when(core == own)
        def _():
            unpack_half(mine_ref[...], halves()[own], gram_ref)
            unpack_half(other_ref[...], halves()[1 - own], gram_ref)
    basis_ref[...] = start_ref[...].T

    def step(_, carry):
        grown = exact(basis_ref[...], gram_ref[...], (1, 0))
        inner = exact(grown, grown, (1, 1))
        basis_ref[...] = exact(inverse_lower(inner), grown, (1, 0))
        return carry

    lax.fori_loop(0, ITERS, step, 0)
    narrow = basis_ref[...].astype(jnp.bfloat16)
    copy.wait()
    src, th, radii, ph = held_ref.shape
    results = []
    for c in range(ph // OUT_CELLS):
        cells = slice(OUT_CELLS * c, OUT_CELLS * (c + 1))
        for t in range(th):
            u = held_ref[:, t, :, cells].reshape(src * radii, OUT_CELLS)
            core_part_ref[:, t, cells] = jnp.dot(narrow, u, preferred_element_type=jnp.float32).astype(jnp.bfloat16)
        part = pl.ds(OUT_CELLS * c, OUT_CELLS)
        results.append(pltpu.make_async_copy(core_part_ref.at[:, :, part], out_ref.at[:, :, part], out_sems.at[c]))
        results[-1].start()
    for result in results:
        result.wait()


def core_of(mine, other, start, held):
    order, rank = start.shape
    src, th, radii, ph = held.shape
    src //= HELD_ROOM
    vmem = pl.BlockSpec(memory_space=pltpu.VMEM)
    return pl.pallas_call(
        core_kernel,
        in_specs=[vmem] * 3 + [pl.BlockSpec(memory_space=pltpu.HBM)],
        out_specs=pl.BlockSpec(memory_space=pltpu.HBM),
        out_shape=jax.ShapeDtypeStruct((rank, th, ph), jnp.bfloat16),
        scratch_shapes=[
            pltpu.VMEM((order, order), jnp.float32),
            pltpu.VMEM((rank, order), jnp.float32),
            pltpu.VMEM((src, th, radii, ph), jnp.bfloat16),
            pltpu.VMEM((rank, th, ph), jnp.bfloat16),
            pltpu.SemaphoreType.DMA,
            pltpu.SemaphoreType.DMA((ph // OUT_CELLS,)),
        ],
        compiler_params=pltpu.CompilerParams(vmem_limit_bytes=VMEM_LIMIT),
        name="subspace_and_core",
    )(mine, other, start, held)


def on_device(field, start):
    radii, th, ph = field.shape
    owners = group(RAD)
    sent = by_colatitude(field).reshape(owners, th // owners, radii, ph)
    regrouped = swap(sent, RAD)
    keep, send, held = partial_gram(regrouped)
    mine, other = sum_everywhere(keep, send)
    return core_of(mine, other, start, held)


def solution(mesh):
    fine = Mesh(mesh.devices.reshape(SIZES), AXES)
    return jax.shard_map(
        on_device,
        mesh=fine,
        in_specs=(P(RAD, ("z", "core"), None), P()),
        out_specs=P(None, ("z", "core") + RAD, None),
        check_vma=False,
    )
```
